32 devices in a mesh: groups: 2 (over x), expert: 8 (over z, y), tensor: 2 (over core).
Axes of the slice: x: 2, y: 2, z: 4, core: 2. Of those that a mesh axis runs over, the one named last changes fastest.
Arguments:
- tokens: bfloat16 [8192, 2048], P(('groups', 'expert', 'tensor')), parts along dimension 0, may hold values from -6 to 6
- routes: int32 [8192, 4], P(('groups', 'expert', 'tensor')), parts along dimension 0, may hold values from 0 to 7, all different within a row; in each aligned block of 256 rows (0 to 255, 256 to 511, ...) at most 128 rows name the same one
- gates: int32 [8192, 4], P(('groups', 'expert', 'tensor')), parts along dimension 0, may hold values from 1 to 4095
- w_gate: bfloat16 [8, 2048, 1408], P('expert', None, 'tensor'), may hold values from -0.125 to 0.125
- w_up: bfloat16 [8, 2048, 1408], P('expert', None, 'tensor'), may hold values from -0.125 to 0.125
- w_down: bfloat16 [8, 1408, 2048], P('expert', 'tensor'), may hold values from -0.15625 to 0.15625
Outputs:
- mixed: bfloat16 [8192, 2048], P(('groups', 'expert', 'tensor')), parts along dimension 0
The draws below stay inside these ranges and needn't reach their ends.
There are 2 independent parts, one for each index of `groups`. The reference program is written for one: setup_inputs(seed, part) draws one part's arguments, and reference() takes and returns one part's arrays. A program takes and returns all parts, laid end to end along the dimension named above; an argument that names none is the same for every part. Nothing has to cross between parts.
Inputs may be any that keep to these rules, and one draw needn't show every extreme that they name: `routes`: each row names 4 different experts. Of one device's 256 rows at most 128 name any one expert, a bound that some block reaches of them.
All inputs are finite; a program needn't handle non-finite values.
Results may differ from the reference program's by a relative error of at most 0.0066.
Values may be sent and summed in bfloat16 or wider, within the bound.
A program may use at most 128 MiB of HBM per device.

```python
import math
import jax
import jax.numpy as jnp
import numpy as np
from jax import lax

D = 2048
HID = 1408
TOPK = 4
TOK_DEV = 256
EXPERTS = 8
CAP = 128
TOKENS = 4096
N_TENSOR = 2


def touch_ends(values, stream_key, smallest, high):
    longest = values.shape.index(max(values.shape))
    spots = []
    for shift in (0, 1):
        where = [jax.random.randint(jax.random.fold_in(stream_key, axis), (), 0, length) for axis, length in enumerate(values.shape)]
        where[longest] = (where[longest] + shift) % values.shape[longest]
        spots.append(tuple(where))
    return values.at[spots[0]].set(smallest).at[spots[1]].set(high)


def shard_levels(own_key, dims, cuts, least, top_value):
    def one(axis_at, parts):
        heights = jax.random.uniform(jax.random.fold_in(jax.random.fold_in(own_key, 6), axis_at), (parts,), jnp.float32, least / len(cuts), top_value / len(cuts))
        return jnp.repeat(jnp.exp(heights), dims[axis_at] // parts).reshape((-1,) + (1,) * (len(dims) - axis_at - 1))

    gain = one(*cuts[0])
    for cut in cuts[1:]:
        gain = gain * one(*cut)
    return gain


def deal_out(own_key, own, number, rows, number_of, top, bound, slope):
    order = jax.random.permutation(own_key, number_of)
    crowded, usual = portions_of(number_of, rows * top, bound, slope, True), portions_of(number_of, rows * top, bound, slope, False)
    places = jnp.arange(number_of)

    def named(sizes, offset_by):
        used = int((sizes > 0).sum())
        fixed = max(1, used // 4)
        shifted = fixed + (places - fixed + offset_by * (used - fixed)) % max(1, number_of - fixed)
        return jnp.zeros((number_of,), jnp.int32).at[order[jnp.where(places < fixed, places, shifted)]].set(jnp.asarray(sizes, jnp.int32))

    sizes = jnp.where(number % 4 == 0, named(crowded, number // 4), named(usual, number - number // 4 - 1))
    mixed = jax.random.permutation(jax.random.fold_in(own, 3), number_of)
    source_of, sink = mixed[0:number_of // 2 * 2:2], mixed[1:number_of // 2 * 2:2]
    room = jnp.minimum(sizes[source_of] - 1, bound - sizes[sink]) // 2
    room = jnp.where((source_of == order[0]) | (sink == order[0]) | (sizes[sink] == 0), 0, jnp.maximum(room, 0))
    shifted = jax.random.randint(jax.random.fold_in(own, 4), (number_of // 2,), 0, 1 << 20) % (room + 1)
    sizes = sizes.at[source_of].add(-shifted).at[sink].add(shifted)
    items = jnp.searchsorted(jnp.cumsum(sizes), jnp.arange(rows * top), side="right").astype(jnp.int32)
    table = items.reshape(top, rows).T
    table = table[jax.random.permutation(jax.random.fold_in(own, 1), rows)]
    offset_by = jax.random.randint(jax.random.fold_in(own, 2), (rows, 1), 0, top)
    return jnp.take_along_axis(table, (jnp.arange(top)[None, :] + offset_by) % top, axis=1)


def portions_of(amount, total, reach, lean, full):
    portions = [(1 << 20) // math.isqrt(standing ** lean) + 1 for standing in range(1, amount + 1)]
    largest = reach if full else min(reach, max(-(-total // amount), total * portions[0] // sum(portions)))
    least = 1 if total - largest >= amount - 1 else 0
    holding, surplus = [largest] + [least] * (amount - 1), total - largest - least * (amount - 1)
    while surplus > 0:
        movable = [i for i in range(1, amount) if holding[i] < largest] or [i for i in range(1, amount) if holding[i] < reach]
        pool, budget = sum([portions[i] for i in movable]), surplus
        for i in movable:
            addition = min(reach - holding[i], max(1, budget * portions[i] // pool), surplus)
            holding[i] = holding[i] + addition
            surplus = surplus - addition
    return np.array(holding)


def scatter_about(stream_key, shape, spread, bound, pieces=(), held_as=jnp.bfloat16):
    gain = shard_levels(stream_key, shape, pieces, -0.22, 0.18) if pieces else 1.0
    entries = jax.random.normal(stream_key, shape, jnp.float32) * spread * gain
    return jnp.minimum(jnp.maximum(entries, -bound), bound).astype(held_as)


def setup_inputs(seed: int = 0, part: int = 0) -> dict:
    keys = jax.random.split(jax.random.key(seed), 7)
    part_splits = jax.random.split(jax.random.fold_in(keys[6], part), 7)
    tokens = scatter_about(part_splits[0], (TOKENS, D), 1.0, 6.0, ((0, 16),))
    routes_keys = jax.random.split(jax.random.fold_in(part_splits[1], 1), TOKENS // TOK_DEV)
    routes_turns = jax.random.permutation(jax.random.fold_in(part_splits[1], 3), TOKENS // TOK_DEV)
    routes = jax.vmap(lambda own, number: deal_out(jax.random.fold_in(part_splits[1], 2), own, number, TOK_DEV, EXPERTS, TOPK, CAP, 2))(routes_keys, routes_turns).reshape((TOKENS, TOPK))
    gates = touch_ends(jax.random.randint(part_splits[2], (TOKENS, TOPK), 1, 4096), jax.random.fold_in(part_splits[2], 1), 1, 4095).astype(jnp.int32)
    w_gate = scatter_about(keys[3], (EXPERTS, D, HID), D ** -0.5, 0.125, ((0, 8), (2, 2)))
    w_up = scatter_about(keys[4], (EXPERTS, D, HID), D ** -0.5, 0.125, ((0, 8), (2, 2)))
    w_down = scatter_about(keys[5], (EXPERTS, HID, D), HID ** -0.5, 0.15625, ((0, 8), (1, 2)))
    return {"tokens": tokens, "routes": routes, "gates": gates, "w_gate": w_gate, "w_up": w_up, "w_down": w_down}


def reference(tokens, routes, gates, w_gate, w_up, w_down):
    pair_expert = routes.reshape(-1)
    pair_count = pair_expert.shape[0]
    token_of = jnp.arange(pair_count, dtype=jnp.int32) // TOPK
    weights = gates.astype(jnp.float32)
    weights = (weights / jnp.sum(weights, axis=1, keepdims=True)).reshape(-1)
    row_limit = EXPERTS * N_TENSOR * CAP
    hid_half = HID // N_TENSOR

    def one_expert(total, expert):
        chosen = pair_expert == expert
        position = jnp.cumsum(chosen.astype(jnp.int32)) - 1
        position = jnp.where(chosen, position, row_limit).astype(jnp.int32)
        picked = jnp.zeros((row_limit,), jnp.int32).at[position].set(token_of, mode="drop")
        pair_weight = jnp.zeros((row_limit,), jnp.float32).at[position].set(weights, mode="drop")
        row_block = tokens[picked]
        gate_act = jnp.dot(row_block, w_gate[expert], preferred_element_type=jnp.float32)
        up_act = jnp.dot(row_block, w_up[expert], preferred_element_type=jnp.float32)
        hidden = (jax.nn.silu(gate_act) * up_act).astype(jnp.bfloat16)
        down_proj = w_down[expert]
        summed = jnp.zeros((row_limit, D), jnp.float32)
        for half_index in range(N_TENSOR):
            partial_value = jnp.dot(hidden[:, half_index * hid_half:(half_index + 1) * hid_half],
                              down_proj[half_index * hid_half:(half_index + 1) * hid_half],
                              preferred_element_type=jnp.float32).astype(jnp.bfloat16)
            summed = summed + lax.optimization_barrier(partial_value).astype(jnp.float32)
        result = lax.optimization_barrier(summed.astype(jnp.bfloat16)).astype(jnp.float32)
        total = total.at[picked].add(pair_weight[:, None] * result)
        return total, None

    total, _ = lax.scan(one_expert, jnp.zeros((TOKENS, D), jnp.float32), jnp.arange(EXPERTS, dtype=jnp.int32))
    return total.astype(jnp.bfloat16)
```

```python
import jax
import jax.numpy as jnp
from jax import lax
from jax.experimental import pallas as pl
from jax.experimental.pallas import tpu as pltpu
from jax.sharding import PartitionSpec as P

TOPK = 4
LINE = 4
CHUNKS = 4
ABSENT = -4096.0
MESH = pl.DeviceIdType.MESH


def moe_kernel(
    tokens_ref, meta_ref, wg_in, wu_in, wd_in, out_ref,
    tok, meta, xbuf, ysend, obuf, retsend, csend, cmb, cmbx, wg, wu, wd, hid,
    own_send, fwd_send, tok_recv, loc_sem, meta_send, meta_recv, w_loc, w_send, w_recv,
    y_send, y_recv, r_send, r_recv, c_send, c_recv, cx_recv,
):
    rows, features = tokens_ref.shape
    half = rows // 2
    width = features // CHUNKS
    experts = meta_ref.shape[0] // 2
    e = lax.axis_index("expert")
    t = lax.axis_index("tensor")
    z = e // 2
    y = e % 2
    e_other = z * 2 + (1 - y)
    h = z // 2
    m = (1 - h) * z + h * (3 - z)
    inner = m == 1
    outer = m == 0
    z_in = z + 1 - 2 * h
    z_out = z - (1 - 2 * h) * m
    src = [(1 - h) * s + h * (3 - s) for s in (m, 1 - m, 2, 3)]

    def zdev(zz):
        return {"expert": zz * 2 + y}

    ydev = {"expert": e_other}
    tdev = {"tensor": 1 - t}

    def remote(a, b, ss, rs, dev):
        return pltpu.make_async_remote_copy(
            src_ref=a, dst_ref=b, send_sem=ss, recv_sem=rs, device_id=dev, device_id_type=MESH
        )

    def cols(c):
        return pl.ds(pl.multiple_of(c * width, width), width)

    barrier = pltpu.get_barrier_semaphore()
    peers = [zdev((z + d) % LINE) for d in range(1, LINE)] + [ydev, tdev]
    for dev in peers:
        pl.semaphore_signal(barrier, inc=1, device_id=dev, device_id_type=MESH)
    pl.semaphore_wait(barrier, len(peers))

    def own_copy(c, dirn):
        return remote(
            tokens_ref.at[:, cols(c)], tok.at[z, c], own_send.at[dirn, c], tok_recv.at[z, c],
            zdev(z_out if dirn else z_in),
        )

    def loc_copy(c):
        return pltpu.make_async_copy(tokens_ref.at[:, cols(c)], tok.at[z, c], loc_sem.at[c])

    def meta_copy(d):
        return remote(
            meta_ref, meta.at[z], meta_send.at[d - 1], meta_recv.at[z], zdev((z + d) % LINE)
        )

    weights = [(wg_in, wg), (wu_in, wu), (wd_in, wd)]

    def w_local(i):
        return pltpu.make_async_copy(weights[i][0].at[0], weights[i][1].at[t], w_loc.at[i])

    def w_remote(i):
        return remote(
            weights[i][0].at[0], weights[i][1].at[t], w_send.at[i], w_recv.at[i], tdev
        )

    def w_arrival(i):
        return remote(
            weights[i][0].at[0], weights[i][1].at[1 - t], w_send.at[i], w_recv.at[i], tdev
        )

    def each(body):
        def step(c, carry):
            body(c)
            return carry

        lax.fori_loop(0, CHUNKS, step, 0)

    def start_own(c):
        loc_copy(c).start()
        own_copy(c, 0).start()

        @pl.when(inner)
        def _():
            own_copy(c, 1).start()

    for d in range(1, LINE):
        meta_copy(d).start()
    each(start_own)
    for i in range(3):
        w_remote(i).start()
        w_local(i).start()
    meta[z] = meta_ref[...]

    def arrival(k, c):
        return remote(
            tokens_ref.at[:, cols(c)], tok.at[src[k], c], own_send.at[0, c],
            tok_recv.at[src[k], c], zdev(z_in),
        )

    def fwd_copy(k, c):
        return remote(
            tok.at[src[k], c], tok.at[src[k], c], fwd_send.at[k - 1, c], tok_recv.at[src[k], c],
            zdev(z_in if k == 1 else z_out),
        )

    def meta_arrival(k):
        return remote(
            meta_ref, meta.at[src[k]], meta_send.at[0], meta_recv.at[src[k]], zdev(z_in)
        )

    def forward(k, c):
        @pl.when(inner)
        def _():
            arrival(k, c).wait_recv()
            fwd_copy(k, c).start()

    slot = lax.broadcasted_iota(jnp.int32, (rows, rows), 0)
    slot_f = slot.astype(jnp.float32)

    def chosen(k):
        rank_own = meta[src[k], pl.ds(e, 1), :]
        rank_other = meta[src[k], pl.ds(e_other, 1), :] + float(half)
        return (slot_f == rank_own) | (slot_f == rank_other)

    def selector(k):
        return jnp.where(chosen(k), 1.0, 0.0).astype(jnp.bfloat16)

    def mixer(k):
        weight = jnp.where(
            slot < half,
            meta[src[k], pl.ds(experts + e, 1), :],
            meta[src[k], pl.ds(experts + e_other, 1), :],
        )
        spread = jnp.where(chosen(k), weight, 0.0).T
        high = spread.astype(jnp.bfloat16)
        low = (spread - high.astype(jnp.float32)).astype(jnp.bfloat16)
        return high, low

    def y_copy(k, c):
        return remote(
            ysend.at[k, c], xbuf.at[k, pl.ds(half, half), cols(c)], y_send.at[k, c],
            y_recv.at[k, c], ydev,
        )

    def r_copy(k, c):
        return remote(
            retsend.at[k, c], obuf.at[k, c, pl.ds(half, half), :], r_send.at[k, c],
            r_recv.at[k, c], ydev,
        )

    def pick(k, c, sel):
        if k == 0:
            loc_copy(c).wait()
        else:
            @pl.when(outer)
            def _():
                arrival(k, c).wait_recv()

        picked = jnp.dot(sel, tok[src[k], c], preferred_element_type=jnp.float32).astype(
            jnp.bfloat16
        )
        xbuf[k, pl.ds(0, half), cols(c)] = picked[:half]
        ysend[k, c] = picked[half:]
        y_copy(k, c).start()

    def ffn(k):
        each(lambda c: y_copy(k, c).wait_recv())
        for i in range(2):
            x = xbuf[k]
            gate = jnp.dot(x, wg[i], preferred_element_type=jnp.float32)
            up = jnp.dot(x, wu[i], preferred_element_type=jnp.float32)
            hid[i] = (jax.nn.silu(gate) * up).astype(jnp.bfloat16)

        def down(c):
            total = jnp.dot(hid[0], wd[0, :, cols(c)], preferred_element_type=jnp.float32)
            total += jnp.dot(hid[1], wd[1, :, cols(c)], preferred_element_type=jnp.float32)
            total = total.astype(jnp.bfloat16)
            obuf[k, c, pl.ds(0, half), :] = total[:half]
            retsend[k, c] = total[half:]
            r_copy(k, c).start()

        each(down)

    def mix(k, c, pair):
        rows_out = obuf[k, c]
        return jnp.dot(pair[0], rows_out, preferred_element_type=jnp.float32) + jnp.dot(
            pair[1], rows_out, preferred_element_type=jnp.float32
        )

    def c_copy(k, c):
        return remote(
            csend.at[k - 1, c], cmb.at[src[k], c], c_send.at[k - 1, c], c_recv.at[src[k], c],
            zdev(z_out if k == 1 else z_in),
        )

    def cx_copy(c):
        return remote(csend.at[0, c], cmbx.at[c], c_send.at[0, c], cx_recv.at[c], zdev(z_in))

    def give(k, c, pair):
        r_copy(k, c).wait_recv()
        total = mix(k, c, pair)

        @pl.when(outer)
        def _():
            csend[k - 1, c] = total.astype(jnp.bfloat16)

        @pl.when(inner)
        def _():
            c_copy(k, c).wait_recv()
            csend[k - 1, c] = (total + cmb[src[k], c].astype(jnp.float32)).astype(jnp.bfloat16)

        c_copy(k, c).start()

    sel0 = selector(0)
    each(lambda c: pick(0, c, sel0))

    meta_arrival(1).wait_recv()
    sel1 = selector(1)

    def near(c):
        forward(1, c)
        forward(2, c)
        pick(1, c, sel1)

    each(near)
    for i in range(3):
        w_local(i).wait()
        w_arrival(i).wait_recv()
    ffn(1)

    @pl.when(outer)
    def _():
        pair = mixer(1)

        def send(c):
            r_copy(1, c).wait_recv()
            csend[0, c] = mix(1, c, pair).astype(jnp.bfloat16)
            cx_copy(c).start()

        each(send)

    meta_arrival(2).wait_recv()
    sel2 = selector(2)
    each(lambda c: pick(2, c, sel2))
    each(lambda c: forward(3, c))
    ffn(0)
    ffn(2)

    meta_arrival(3).wait_recv()
    sel3 = selector(3)
    pair2 = mixer(2)

    def far(c):
        pick(3, c, sel3)
        give(2, c, pair2)

    each(far)
    ffn(3)
    pair3 = mixer(3)
    each(lambda c: give(3, c, pair3))

    @pl.when(inner)
    def _():
        pair = mixer(1)

        def send(c):
            r_copy(1, c).wait_recv()
            total = mix(1, c, pair)
            c_copy(1, c).wait_recv()
            csend[0, c] = (total + cmb[src[1], c].astype(jnp.float32)).astype(jnp.bfloat16)
            c_copy(1, c).start()

        each(send)

    pair0 = mixer(0)

    def finish(c):
        r_copy(0, c).wait_recv()
        total = mix(0, c, pair0)
        remote(
            csend.at[0, c], cmb.at[z, c], c_send.at[0, c], c_recv.at[z, c], zdev(z_in)
        ).wait_recv()
        total = total + cmb[z, c].astype(jnp.float32)

        @pl.when(outer)
        def _():
            out_ref[:, cols(c)] = total.astype(jnp.bfloat16)

        @pl.when(inner)
        def _():
            cx_copy(c).wait_recv()
            out_ref[:, cols(c)] = (total + cmbx[c].astype(jnp.float32)).astype(jnp.bfloat16)

    each(finish)

    def drain(c):
        own_copy(c, 0).wait_send()
        for k in range(LINE):
            y_copy(k, c).wait_send()
            r_copy(k, c).wait_send()
        for k in (2, 3):
            c_copy(k, c).wait_send()

        @pl.when(inner)
        def _():
            own_copy(c, 1).wait_send()
            for k in (1, 2, 3):
                fwd_copy(k, c).wait_send()
            c_copy(1, c).wait_send()

        @pl.when(outer)
        def _():
            cx_copy(c).wait_send()

    each(drain)
    for d in range(1, LINE):
        meta_copy(d).wait_send()
    for i in range(3):
        w_remote(i).wait_send()


def fused(tokens, routes, gates, w_gate, w_up, w_down):
    rows, features = tokens.shape
    experts = lax.axis_size("expert")
    half, width = rows // 2, features // CHUNKS
    hidden = w_gate.shape[2]
    weights = gates.astype(jnp.float32)
    weights = weights / jnp.sum(weights, axis=1, keepdims=True)
    names = routes[:, :, None] == jnp.arange(experts, dtype=jnp.int32)[None, None, :]
    weight_of = jnp.sum(jnp.where(names, weights[:, :, None], 0.0), axis=1).T
    chosen = jnp.any(names, axis=1).T
    place = jnp.arange(rows, dtype=jnp.int32)
    earlier = (place[:, None] < place[None, :]).astype(jnp.bfloat16)
    rank = jnp.dot(chosen.astype(jnp.bfloat16), earlier, preferred_element_type=jnp.float32)
    meta = jnp.concatenate([jnp.where(chosen, rank, ABSENT), weight_of], axis=0)
    bf16, dma = jnp.bfloat16, pltpu.SemaphoreType.DMA
    return pl.pallas_call(
        moe_kernel,
        out_shape=jax.ShapeDtypeStruct((rows, features), bf16),
        in_specs=[
            pl.BlockSpec(memory_space=pl.ANY),
            pl.BlockSpec(memory_space=pltpu.VMEM),
            pl.BlockSpec(memory_space=pl.ANY),
            pl.BlockSpec(memory_space=pl.ANY),
            pl.BlockSpec(memory_space=pl.ANY),
        ],
        out_specs=pl.BlockSpec(memory_space=pltpu.VMEM),
        scratch_shapes=[
            pltpu.VMEM((LINE, CHUNKS, rows, width), bf16),
            pltpu.VMEM((LINE, 2 * experts, rows), jnp.float32),
            pltpu.VMEM((LINE, rows, features), bf16),
            pltpu.VMEM((LINE, CHUNKS, half, width), bf16),
            pltpu.VMEM((LINE, CHUNKS, rows, width), bf16),
            pltpu.VMEM((LINE, CHUNKS, half, width), bf16),
            pltpu.VMEM((LINE - 1, CHUNKS, rows, width), bf16),
            pltpu.VMEM((LINE, CHUNKS, rows, width), bf16),
            pltpu.VMEM((CHUNKS, rows, width), bf16),
            pltpu.VMEM((2, features, hidden), bf16),
            pltpu.VMEM((2, features, hidden), bf16),
            pltpu.VMEM((2, hidden, features), bf16),
            pltpu.VMEM((2, rows, hidden), bf16),
            dma((2, CHUNKS)),
            dma((LINE - 1, CHUNKS)),
            dma((LINE, CHUNKS)),
            dma((CHUNKS,)),
            dma((LINE - 1,)),
            dma((LINE,)),
            dma((3,)),
            dma((3,)),
            dma((3,)),
            dma((LINE, CHUNKS)),
            dma((LINE, CHUNKS)),
            dma((LINE, CHUNKS)),
            dma((LINE, CHUNKS)),
            dma((LINE - 1, CHUNKS)),
            dma((LINE, CHUNKS)),
            dma((CHUNKS,)),
        ],
        compiler_params=pltpu.CompilerParams(
            collective_id=0, has_side_effects=True, vmem_limit_bytes=56 * 1024 * 1024
        ),
        name="moe",
    )(tokens, meta, w_gate, w_up, w_down)


def swiglu(row_block, gate_proj, up_proj):
    gate_act = jnp.dot(row_block, gate_proj, preferred_element_type=jnp.float32)
    up_act = jnp.dot(row_block, up_proj, preferred_element_type=jnp.float32)
    return (jax.nn.silu(gate_act) * up_act).astype(jnp.bfloat16)


def rounded_term(hidden, down_proj):
    return jnp.dot(hidden, down_proj, preferred_element_type=jnp.float32).astype(jnp.bfloat16)


def on_device(tokens, routes, gates, w_gate, w_up, w_down):
    tok_dev, features = tokens.shape
    experts = lax.axis_size("expert")
    capacity = max(5 * tok_dev // 16, TOPK * tok_dev // experts)
    gate_proj = w_gate[0]
    up_proj = w_up[0]
    down_proj = w_down[0]
    pair_expert = routes.reshape(-1)
    onehot = (pair_expert[:, None] == jnp.arange(experts, dtype=jnp.int32)[None, :]).astype(
        jnp.int32
    )
    rank_in = jnp.sum((jnp.cumsum(onehot, axis=0) - onehot) * onehot, axis=1)
    slot_index = (pair_expert * capacity + rank_in).reshape(tok_dev, TOPK)
    all_slots = jnp.arange(experts * capacity, dtype=jnp.int32)
    selector = jnp.any(slot_index[None, :, :] == all_slots[:, None, None], axis=2).astype(
        jnp.bfloat16
    )
    outgoing = jnp.dot(selector, tokens, preferred_element_type=jnp.float32).astype(jnp.bfloat16)
    outgoing = outgoing.reshape(experts, capacity, features)
    arrived = lax.all_to_all(outgoing, "expert", split_axis=0, concat_axis=0, tiled=True)
    hidden = swiglu(
        lax.all_gather(arrived.reshape(experts * capacity, features), "tensor", axis=0, tiled=True),
        gate_proj,
        up_proj,
    )
    term = lax.optimization_barrier(rounded_term(hidden, down_proj))
    summed = lax.psum_scatter(
        term.astype(jnp.float32).astype(jnp.bfloat16), "tensor", scatter_dimension=0, tiled=True
    )
    outputs = summed.reshape(experts, capacity, features)
    returned = lax.all_to_all(outputs, "expert", split_axis=0, concat_axis=0, tiled=True)
    weights = gates.astype(jnp.float32)
    weights = weights / jnp.sum(weights, axis=1, keepdims=True)
    flat_back = returned.reshape(experts * capacity, features)
    picked = jnp.take(flat_back, slot_index.reshape(-1), axis=0).reshape(tok_dev, TOPK, features)
    mixed = jnp.sum(picked.astype(jnp.float32) * weights[:, :, None], axis=1)
    return mixed.astype(jnp.bfloat16)


def solution(mesh):
    in_specs = (
        P(("groups", "expert", "tensor"), None),
        P(("groups", "expert", "tensor"), None),
        P(("groups", "expert", "tensor"), None),
        P("expert", None, "tensor"),
        P("expert", None, "tensor"),
        P("expert", "tensor", None),
    )
    out_specs = P(("groups", "expert", "tensor"), None)
    paired = mesh.shape["expert"] == 2 * LINE and mesh.shape["tensor"] == 2
    return jax.shard_map(
        fused if paired else on_device, mesh=mesh, in_specs=in_specs, out_specs=out_specs, check_vma=False
    )
```

```python
import jax
import jax.numpy as jnp
from jax import lax
from jax.experimental import pallas as pl
from jax.experimental.pallas import tpu as pltpu
from jax.sharding import PartitionSpec as P

TOPK = 4
LINE = 4
CHUNKS = 4
ABSENT = -4096.0
LAST = (((1,), (1,)), ((), ()))
MESH = pl.DeviceIdType.MESH


def moe_kernel(
    tokens_ref, routes_ref, gates_ref, wg_in, wu_in, wd_in, out_ref,
    tok, meta, xbuf, ysend, obuf, retsend, csend, cmb, cmbx, wg, wu, wd, hid,
    own_send, fwd_send, tok_recv, loc_sem, meta_send, meta_recv, w_loc, w_send, w_recv,
    y_send, y_recv, r_send, r_recv, c_send, c_recv, cx_recv,
):
    rows, features = tokens_ref.shape
    half = rows // 2
    width = features // CHUNKS
    experts = meta.shape[1] // 2
    e = lax.axis_index("expert")
    t = lax.axis_index("tensor")
    z = e // 2
    y = e % 2
    e_other = z * 2 + (1 - y)
    h = z // 2
    m = (1 - h) * z + h * (3 - z)
    inner = m == 1
    outer = m == 0
    z_in = z + 1 - 2 * h
    z_out = z - (1 - 2 * h) * m
    src = [(1 - h) * s + h * (3 - s) for s in (m, 1 - m, 2, 3)]

    def zdev(zz):
        return {"expert": zz * 2 + y}

    ydev = {"expert": e_other}
    tdev = {"tensor": 1 - t}

    def remote(a, b, ss, rs, dev):
        return pltpu.make_async_remote_copy(
            src_ref=a, dst_ref=b, send_sem=ss, recv_sem=rs, device_id=dev, device_id_type=MESH
        )

    def cols(c):
        return pl.ds(pl.multiple_of(c * width, width), width)

    barrier = pltpu.get_barrier_semaphore()
    peers = [zdev((z + d) % LINE) for d in range(1, LINE)] + [ydev, tdev]
    for dev in peers:
        pl.semaphore_signal(barrier, inc=1, device_id=dev, device_id_type=MESH)
    pl.semaphore_wait(barrier, len(peers))

    def own_copy(c, dirn):
        return remote(
            tokens_ref.at[:, cols(c)], tok.at[z, c], own_send.at[dirn, c], tok_recv.at[z, c],
            zdev(z_out if dirn else z_in),
        )

    def loc_copy(c):
        return pltpu.make_async_copy(tokens_ref.at[:, cols(c)], tok.at[z, c], loc_sem.at[c])

    def meta_copy(d):
        return remote(
            meta.at[z], meta.at[z], meta_send.at[d - 1], meta_recv.at[z], zdev((z + d) % LINE)
        )

    weights = [(wg_in, wg), (wu_in, wu), (wd_in, wd)]

    def w_local(i):
        return pltpu.make_async_copy(weights[i][0], weights[i][1].at[t], w_loc.at[i])

    def w_remote(i):
        return remote(
            weights[i][0], weights[i][1].at[t], w_send.at[i], w_recv.at[i], tdev
        )

    def w_arrival(i):
        return remote(
            weights[i][0], weights[i][1].at[1 - t], w_send.at[i], w_recv.at[i], tdev
        )

    def each(body):
        def step(c, carry):
            body(c)
            return carry

        lax.fori_loop(0, CHUNKS, step, 0)

    def start_own(c):
        loc_copy(c).start()
        own_copy(c, 0).start()

        @pl.when(inner)
        def _():
            own_copy(c, 1).start()

    each(start_own)
    for i in range(3):
        w_remote(i).start()
        w_local(i).start()

    gate = gates_ref[...].astype(jnp.float32)
    gate = gate / jnp.sum(gate, axis=0, keepdims=True)
    expert_of = lax.broadcasted_iota(jnp.int32, (experts, rows), 0)
    weight_of = jnp.zeros((experts, rows), jnp.float32)
    named = jnp.zeros((experts, rows), jnp.float32)
    for k in range(TOPK):
        match = expert_of == routes_ref[k : k + 1, :]
        weight_of = jnp.where(match, gate[k : k + 1, :], weight_of)
        named = jnp.where(match, 1.0, named)
    before = lax.broadcasted_iota(jnp.int32, (rows, rows), 0)
    after = lax.broadcasted_iota(jnp.int32, (rows, rows), 1)
    earlier = jnp.where(before < after, 1.0, 0.0).astype(jnp.bfloat16)
    rank = jnp.dot(named.astype(jnp.bfloat16), earlier, preferred_element_type=jnp.float32)
    meta[z, pl.ds(0, experts), :] = jnp.where(named > 0.5, rank, ABSENT)
    meta[z, pl.ds(experts, experts), :] = weight_of
    for d in range(1, LINE):
        meta_copy(d).start()

    def arrival(k, c):
        return remote(
            tokens_ref.at[:, cols(c)], tok.at[src[k], c], own_send.at[0, c],
            tok_recv.at[src[k], c], zdev(z_in),
        )

    def fwd_copy(k, c):
        return remote(
            tok.at[src[k], c], tok.at[src[k], c], fwd_send.at[k - 1, c], tok_recv.at[src[k], c],
            zdev(z_in if k == 1 else z_out),
        )

    def meta_arrival(k):
        return remote(
            meta.at[z], meta.at[src[k]], meta_send.at[0], meta_recv.at[src[k]], zdev(z_in)
        )

    def forward(k, c):
        @pl.when(inner)
        def _():
            arrival(k, c).wait_recv()
            fwd_copy(k, c).start()

    slot = lax.broadcasted_iota(jnp.int32, (rows, rows), 0)
    slot_f = slot.astype(jnp.float32)

    def chosen(k):
        rank_own = meta[src[k], pl.ds(e, 1), :]
        rank_other = meta[src[k], pl.ds(e_other, 1), :] + float(half)
        return (slot_f == rank_own) | (slot_f == rank_other)

    def selector(k):
        return jnp.where(chosen(k), 1.0, 0.0).astype(jnp.bfloat16)

    def mixer(k):
        weight = jnp.where(
            slot < half,
            meta[src[k], pl.ds(experts + e, 1), :],
            meta[src[k], pl.ds(experts + e_other, 1), :],
        )
        spread = jnp.where(chosen(k), weight, 0.0).T
        high = spread.astype(jnp.bfloat16)
        low = (spread - high.astype(jnp.float32)).astype(jnp.bfloat16)
        return high, low

    def y_copy(k, c):
        return remote(
            ysend.at[k, c], xbuf.at[k, pl.ds(half, half), cols(c)], y_send.at[k, c],
            y_recv.at[k, c], ydev,
        )

    def r_copy(k, c):
        return remote(
            retsend.at[k, c], obuf.at[k, c, pl.ds(half, half), :], r_send.at[k, c],
            r_recv.at[k, c], ydev,
        )

    def pick(k, c, sel):
        if k == 0:
            loc_copy(c).wait()
        else:
            @pl.when(outer)
            def _():
                arrival(k, c).wait_recv()

        picked = jnp.dot(sel, tok[src[k], c], preferred_element_type=jnp.float32).astype(
            jnp.bfloat16
        )
        xbuf[k, pl.ds(0, half), cols(c)] = picked[:half]
        ysend[k, c] = picked[half:]
        y_copy(k, c).start()

    def ffn(k):
        each(lambda c: y_copy(k, c).wait_recv())
        for i in range(2):
            x = xbuf[k]
            gate = lax.dot_general(x, wg[i], LAST, preferred_element_type=jnp.float32)
            up = lax.dot_general(x, wu[i], LAST, preferred_element_type=jnp.float32)
            hid[i] = (jax.nn.silu(gate) * up).astype(jnp.bfloat16)

        def down(c):
            total = jnp.dot(hid[0], wd[0, :, cols(c)], preferred_element_type=jnp.float32)
            total += jnp.dot(hid[1], wd[1, :, cols(c)], preferred_element_type=jnp.float32)
            total = total.astype(jnp.bfloat16)
            obuf[k, c, pl.ds(0, half), :] = total[:half]
            retsend[k, c] = total[half:]
            r_copy(k, c).start()

        each(down)

    def mix(k, c, pair):
        rows_out = obuf[k, c]
        return jnp.dot(pair[0], rows_out, preferred_element_type=jnp.float32) + jnp.dot(
            pair[1], rows_out, preferred_element_type=jnp.float32
        )

    def c_copy(k, c):
        return remote(
            csend.at[k - 1, c], cmb.at[src[k], c], c_send.at[k - 1, c], c_recv.at[src[k], c],
            zdev(z_out if k == 1 else z_in),
        )

    def cx_copy(c):
        return remote(csend.at[0, c], cmbx.at[c], c_send.at[0, c], cx_recv.at[c], zdev(z_in))

    def give(k, c, pair):
        r_copy(k, c).wait_recv()
        total = mix(k, c, pair)

        @pl.when(outer)
        def _():
            csend[k - 1, c] = total.astype(jnp.bfloat16)

        @pl.when(inner)
        def _():
            c_copy(k, c).wait_recv()
            csend[k - 1, c] = (total + cmb[src[k], c].astype(jnp.float32)).astype(jnp.bfloat16)

        c_copy(k, c).start()

    sel0 = selector(0)
    each(lambda c: pick(0, c, sel0))

    meta_arrival(1).wait_recv()
    sel1 = selector(1)

    def near(c):
        forward(1, c)
        forward(2, c)
        pick(1, c, sel1)

    each(near)
    for i in range(3):
        w_local(i).wait()
        w_arrival(i).wait_recv()
    ffn(1)

    meta_arrival(2).wait_recv()
    sel2 = selector(2)
    pair1 = mixer(1)

    def second(c):
        @pl.when(outer)
        def _():
            r_copy(1, c).wait_recv()
            csend[0, c] = mix(1, c, pair1).astype(jnp.bfloat16)
            cx_copy(c).start()

        pick(2, c, sel2)

    each(second)
    each(lambda c: forward(3, c))
    ffn(2)

    meta_arrival(3).wait_recv()
    sel3 = selector(3)
    pair2 = mixer(2)

    def far(c):
        pick(3, c, sel3)
        give(2, c, pair2)

    each(far)
    ffn(3)
    pair3 = mixer(3)

    @pl.when(outer)
    def _():
        each(lambda c: give(3, c, pair3))
        ffn(0)

    @pl.when(inner)
    def _():
        ffn(0)

        def last_hop(c):
            r_copy(1, c).wait_recv()
            total = mix(1, c, pair1)
            c_copy(1, c).wait_recv()
            csend[0, c] = (total + cmb[src[1], c].astype(jnp.float32)).astype(jnp.bfloat16)
            c_copy(1, c).start()

        give(3, 0, pair3)

        def step(c, carry):
            give(3, c, pair3)
            last_hop(c - 1)
            return carry

        lax.fori_loop(1, CHUNKS, step, 0)
        last_hop(CHUNKS - 1)

    pair0 = mixer(0)

    def finish(c):
        r_copy(0, c).wait_recv()
        total = mix(0, c, pair0)
        remote(
            csend.at[0, c], cmb.at[z, c], c_send.at[0, c], c_recv.at[z, c], zdev(z_in)
        ).wait_recv()
        total = total + cmb[z, c].astype(jnp.float32)

        @pl.when(outer)
        def _():
            out_ref[:, cols(c)] = total.astype(jnp.bfloat16)

        @pl.when(inner)
        def _():
            cx_copy(c).wait_recv()
            out_ref[:, cols(c)] = (total + cmbx[c].astype(jnp.float32)).astype(jnp.bfloat16)

    each(finish)

    def drain(c):
        own_copy(c, 0).wait_send()
        for k in range(LINE):
            y_copy(k, c).wait_send()
            r_copy(k, c).wait_send()
        for k in (2, 3):
            c_copy(k, c).wait_send()

        @pl.when(inner)
        def _():
            own_copy(c, 1).wait_send()
            for k in (1, 2, 3):
                fwd_copy(k, c).wait_send()
            c_copy(1, c).wait_send()

        @pl.when(outer)
        def _():
            cx_copy(c).wait_send()

    each(drain)
    for d in range(1, LINE):
        meta_copy(d).wait_send()
    for i in range(3):
        w_remote(i).wait_send()


def fused(tokens, routes, gates, w_gate, w_up, w_down):
    rows, features = tokens.shape
    experts = lax.axis_size("expert")
    half, width = rows // 2, features // CHUNKS
    hidden = w_gate.shape[2]
    bf16, dma = jnp.bfloat16, pltpu.SemaphoreType.DMA
    return pl.pallas_call(
        moe_kernel,
        out_shape=jax.ShapeDtypeStruct((rows, features), bf16),
        in_specs=[
            pl.BlockSpec(memory_space=pl.ANY),
            pl.BlockSpec(memory_space=pltpu.VMEM),
            pl.BlockSpec(memory_space=pltpu.VMEM),
            pl.BlockSpec(memory_space=pl.ANY),
            pl.BlockSpec(memory_space=pl.ANY),
            pl.BlockSpec(memory_space=pl.ANY),
        ],
        out_specs=pl.BlockSpec(memory_space=pltpu.VMEM),
        scratch_shapes=[
            pltpu.VMEM((LINE, CHUNKS, rows, width), bf16),
            pltpu.VMEM((LINE, 2 * experts, rows), jnp.float32),
            pltpu.VMEM((LINE, rows, features), bf16),
            pltpu.VMEM((LINE, CHUNKS, half, width), bf16),
            pltpu.VMEM((LINE, CHUNKS, rows, width), bf16),
            pltpu.VMEM((LINE, CHUNKS, half, width), bf16),
            pltpu.VMEM((LINE - 1, CHUNKS, rows, width), bf16),
            pltpu.VMEM((LINE, CHUNKS, rows, width), bf16),
            pltpu.VMEM((CHUNKS, rows, width), bf16),
            pltpu.VMEM((2, hidden, features), bf16),
            pltpu.VMEM((2, hidden, features), bf16),
            pltpu.VMEM((2, hidden, features), bf16),
            pltpu.VMEM((2, rows, hidden), bf16),
            dma((2, CHUNKS)),
            dma((LINE - 1, CHUNKS)),
            dma((LINE, CHUNKS)),
            dma((CHUNKS,)),
            dma((LINE - 1,)),
            dma((LINE,)),
            dma((3,)),
            dma((3,)),
            dma((3,)),
            dma((LINE, CHUNKS)),
            dma((LINE, CHUNKS)),
            dma((LINE, CHUNKS)),
            dma((LINE, CHUNKS)),
            dma((LINE - 1, CHUNKS)),
            dma((LINE, CHUNKS)),
            dma((CHUNKS,)),
        ],
        compiler_params=pltpu.CompilerParams(
            collective_id=0, has_side_effects=True, vmem_limit_bytes=56 * 1024 * 1024
        ),
        name="moe",
    )(tokens, routes.T, gates.T, w_gate[0].T, w_up[0].T, w_down[0])


def swiglu(row_block, gate_proj, up_proj):
    gate_act = jnp.dot(row_block, gate_proj, preferred_element_type=jnp.float32)
    up_act = jnp.dot(row_block, up_proj, preferred_element_type=jnp.float32)
    return (jax.nn.silu(gate_act) * up_act).astype(jnp.bfloat16)


def rounded_term(hidden, down_proj):
    return jnp.dot(hidden, down_proj, preferred_element_type=jnp.float32).astype(jnp.bfloat16)


def on_device(tokens, routes, gates, w_gate, w_up, w_down):
    tok_dev, features = tokens.shape
    experts = lax.axis_size("expert")
    capacity = max(5 * tok_dev // 16, TOPK * tok_dev // experts)
    gate_proj = w_gate[0]
    up_proj = w_up[0]
    down_proj = w_down[0]
    pair_expert = routes.reshape(-1)
    onehot = (pair_expert[:, None] == jnp.arange(experts, dtype=jnp.int32)[None, :]).astype(
        jnp.int32
    )
    rank_in = jnp.sum((jnp.cumsum(onehot, axis=0) - onehot) * onehot, axis=1)
    slot_index = (pair_expert * capacity + rank_in).reshape(tok_dev, TOPK)
    all_slots = jnp.arange(experts * capacity, dtype=jnp.int32)
    selector = jnp.any(slot_index[None, :, :] == all_slots[:, None, None], axis=2).astype(
        jnp.bfloat16
    )
    outgoing = jnp.dot(selector, tokens, preferred_element_type=jnp.float32).astype(jnp.bfloat16)
    outgoing = outgoing.reshape(experts, capacity, features)
    arrived = lax.all_to_all(outgoing, "expert", split_axis=0, concat_axis=0, tiled=True)
    hidden = swiglu(
        lax.all_gather(arrived.reshape(experts * capacity, features), "tensor", axis=0, tiled=True),
        gate_proj,
        up_proj,
    )
    term = lax.optimization_barrier(rounded_term(hidden, down_proj))
    summed = lax.psum_scatter(
        term.astype(jnp.float32).astype(jnp.bfloat16), "tensor", scatter_dimension=0, tiled=True
    )
    outputs = summed.reshape(experts, capacity, features)
    returned = lax.all_to_all(outputs, "expert", split_axis=0, concat_axis=0, tiled=True)
    weights = gates.astype(jnp.float32)
    weights = weights / jnp.sum(weights, axis=1, keepdims=True)
    flat_back = returned.reshape(experts * capacity, features)
    picked = jnp.take(flat_back, slot_index.reshape(-1), axis=0).reshape(tok_dev, TOPK, features)
    mixed = jnp.sum(picked.astype(jnp.float32) * weights[:, :, None], axis=1)
    return mixed.astype(jnp.bfloat16)


def solution(mesh):
    in_specs = (
        P(("groups", "expert", "tensor"), None),
        P(("groups", "expert", "tensor"), None),
        P(("groups", "expert", "tensor"), None),
        P("expert", None, "tensor"),
        P("expert", None, "tensor"),
        P("expert", "tensor", None),
    )
    out_specs = P(("groups", "expert", "tensor"), None)
    paired = mesh.shape["expert"] == 2 * LINE and mesh.shape["tensor"] == 2
    return jax.shard_map(
        fused if paired else on_device, mesh=mesh, in_specs=in_specs, out_specs=out_specs, check_vma=False
    )
```

```python
import jax
import jax.numpy as jnp
from jax import lax
from jax.experimental import pallas as pl
from jax.experimental.pallas import tpu as pltpu
from jax.sharding import PartitionSpec as P

TOPK = 4
LINE = 4
CHUNKS = 4
ABSENT = -4096.0
LAST = (((1,), (1,)), ((), ()))
MESH = pl.DeviceIdType.MESH


def moe_kernel(
    tokens_ref, routes_ref, gates_ref, wg_in, wu_in, wd_in, out_ref,
    tok, meta, xbuf, ysend, obuf, retsend, csend, cmb, cmbx, wg, wu, wd, hid,
    own_send, fwd_send, tok_recv, loc_sem, meta_send, meta_recv, w_loc, w_send, w_recv,
    y_send, y_recv, r_send, r_recv, c_send, c_recv, cx_recv,
):
    rows, features = tokens_ref.shape
    half = rows // 2
    width = features // CHUNKS
    experts = meta.shape[1] // 2
    e = lax.axis_index("expert")
    t = lax.axis_index("tensor")
    z = e // 2
    y = e % 2
    e_other = z * 2 + (1 - y)
    h = z // 2
    m = (1 - h) * z + h * (3 - z)
    inner = m == 1
    outer = m == 0
    z_in = z + 1 - 2 * h
    z_out = z - (1 - 2 * h) * m
    src = [(1 - h) * s + h * (3 - s) for s in (m, 1 - m, 2, 3)]

    def zdev(zz):
        return {"expert": zz * 2 + y}

    ydev = {"expert": e_other}
    tdev = {"tensor": 1 - t}

    def remote(a, b, ss, rs, dev):
        return pltpu.make_async_remote_copy(
            src_ref=a, dst_ref=b, send_sem=ss, recv_sem=rs, device_id=dev, device_id_type=MESH
        )

    def cols(c):
        return pl.ds(pl.multiple_of(c * width, width), width)

    barrier = pltpu.get_barrier_semaphore()
    peers = [zdev((z + d) % LINE) for d in range(1, LINE)] + [ydev, tdev]
    for dev in peers:
        pl.semaphore_signal(barrier, inc=1, device_id=dev, device_id_type=MESH)
    pl.semaphore_wait(barrier, len(peers))

    def own_copy(c, dirn):
        return remote(
            tokens_ref.at[:, cols(c)], tok.at[z, c], own_send.at[dirn, c], tok_recv.at[z, c],
            zdev(z_out if dirn else z_in),
        )

    def loc_copy(c):
        return pltpu.make_async_copy(tokens_ref.at[:, cols(c)], tok.at[z, c], loc_sem.at[c])

    def meta_copy(d):
        return remote(
            meta.at[z], meta.at[z], meta_send.at[d - 1], meta_recv.at[z], zdev((z + d) % LINE)
        )

    weights = [(wg_in, wg), (wu_in, wu), (wd_in, wd)]

    def w_local(i):
        return pltpu.make_async_copy(weights[i][0], weights[i][1].at[t], w_loc.at[i])

    def w_remote(i):
        return remote(
            weights[i][0], weights[i][1].at[t], w_send.at[i], w_recv.at[i], tdev
        )

    def w_arrival(i):
        return remote(
            weights[i][0], weights[i][1].at[1 - t], w_send.at[i], w_recv.at[i], tdev
        )

    def each(body):
        def step(c, carry):
            body(c)
            return carry

        lax.fori_loop(0, CHUNKS, step, 0)

    def start_own(c):
        loc_copy(c).start()
        own_copy(c, 0).start()

        @pl.when(inner)
        def _():
            own_copy(c, 1).start()

    each(start_own)
    for i in range(3):
        w_remote(i).start()
        w_local(i).start()

    gate = gates_ref[...].astype(jnp.float32)
    gate = gate / jnp.sum(gate, axis=0, keepdims=True)
    expert_of = lax.broadcasted_iota(jnp.int32, (experts, rows), 0)
    weight_of = jnp.zeros((experts, rows), jnp.float32)
    named = jnp.zeros((experts, rows), jnp.float32)
    for k in range(TOPK):
        match = expert_of == routes_ref[k : k + 1, :]
        weight_of = jnp.where(match, gate[k : k + 1, :], weight_of)
        named = jnp.where(match, 1.0, named)
    before = lax.broadcasted_iota(jnp.int32, (rows, rows), 0)
    after = lax.broadcasted_iota(jnp.int32, (rows, rows), 1)
    earlier = jnp.where(before < after, 1.0, 0.0).astype(jnp.bfloat16)
    rank = jnp.dot(named.astype(jnp.bfloat16), earlier, preferred_element_type=jnp.float32)
    meta[z, pl.ds(0, experts), :] = jnp.where(named > 0.5, rank, ABSENT)
    meta[z, pl.ds(experts, experts), :] = weight_of
    for d in range(1, LINE):
        meta_copy(d).start()

    def arrival(k, c):
        return remote(
            tokens_ref.at[:, cols(c)], tok.at[src[k], c], own_send.at[0, c],
            tok_recv.at[src[k], c], zdev(z_in),
        )

    def fwd_copy(k, c):
        return remote(
            tok.at[src[k], c], tok.at[src[k], c], fwd_send.at[k - 1, c], tok_recv.at[src[k], c],
            zdev(z_in if k == 1 else z_out),
        )

    def meta_arrival(k):
        return remote(
            meta.at[z], meta.at[src[k]], meta_send.at[0], meta_recv.at[src[k]], zdev(z_in)
        )

    def forward(k, c):
        @pl.when(inner)
        def _():
            arrival(k, c).wait_recv()
            fwd_copy(k, c).start()

    slot = lax.broadcasted_iota(jnp.int32, (rows, rows), 0)
    slot_f = slot.astype(jnp.float32)

    def chosen(k):
        rank_own = meta[src[k], pl.ds(e, 1), :]
        rank_other = meta[src[k], pl.ds(e_other, 1), :] + float(half)
        return (slot_f == rank_own) | (slot_f == rank_other)

    def selector(k):
        return jnp.where(chosen(k), 1.0, 0.0).astype(jnp.bfloat16)

    def mixer(k):
        weight = jnp.where(
            slot < half,
            meta[src[k], pl.ds(experts + e, 1), :],
            meta[src[k], pl.ds(experts + e_other, 1), :],
        )
        spread = jnp.where(chosen(k), weight, 0.0).T
        high = spread.astype(jnp.bfloat16)
        low = (spread - high.astype(jnp.float32)).astype(jnp.bfloat16)
        return high, low

    def y_copy(k, c):
        return remote(
            ysend.at[k, c], xbuf.at[k, pl.ds(half, half), cols(c)], y_send.at[k, c],
            y_recv.at[k, c], ydev,
        )

    def r_copy(k, c):
        return remote(
            retsend.at[k, c], obuf.at[k, c, pl.ds(half, half), :], r_send.at[k, c],
            r_recv.at[k, c], ydev,
        )

    def pick(k, c, sel):
        if k == 0:
            loc_copy(c).wait()
        else:
            @pl.when(outer)
            def _():
                arrival(k, c).wait_recv()

        picked = jnp.dot(sel, tok[src[k], c], preferred_element_type=jnp.float32).astype(
            jnp.bfloat16
        )
        xbuf[k, pl.ds(0, half), cols(c)] = picked[:half]
        ysend[k, c] = picked[half:]
        y_copy(k, c).start()

    def ffn(k):
        each(lambda c: y_copy(k, c).wait_recv())
        for i in range(2):
            x = xbuf[k]
            gate = lax.dot_general(wg[i], x, LAST, preferred_element_type=jnp.float32)
            up = lax.dot_general(wu[i], x, LAST, preferred_element_type=jnp.float32)
            hid[i] = (jax.nn.silu(gate) * up).T.astype(jnp.bfloat16)

        def down(c):
            total = jnp.dot(hid[0], wd[0, :, cols(c)], preferred_element_type=jnp.float32)
            total += jnp.dot(hid[1], wd[1, :, cols(c)], preferred_element_type=jnp.float32)
            total = total.astype(jnp.bfloat16)
            obuf[k, c, pl.ds(0, half), :] = total[:half]
            retsend[k, c] = total[half:]
            r_copy(k, c).start()

        each(down)

    def mix(k, c, pair):
        rows_out = obuf[k, c]
        return jnp.dot(pair[0], rows_out, preferred_element_type=jnp.float32) + jnp.dot(
            pair[1], rows_out, preferred_element_type=jnp.float32
        )

    def c_copy(k, c):
        return remote(
            csend.at[k - 1, c], cmb.at[src[k], c], c_send.at[k - 1, c], c_recv.at[src[k], c],
            zdev(z_out if k == 1 else z_in),
        )

    def cx_copy(c):
        return remote(csend.at[0, c], cmbx.at[c], c_send.at[0, c], cx_recv.at[c], zdev(z_in))

    def give(k, c, pair):
        r_copy(k, c).wait_recv()
        total = mix(k, c, pair)

        @pl.when(outer)
        def _():
            csend[k - 1, c] = total.astype(jnp.bfloat16)

        @pl.when(inner)
        def _():
            c_copy(k, c).wait_recv()
            csend[k - 1, c] = (total + cmb[src[k], c].astype(jnp.float32)).astype(jnp.bfloat16)

        c_copy(k, c).start()

    sel0 = selector(0)
    each(lambda c: pick(0, c, sel0))

    meta_arrival(1).wait_recv()
    sel1 = selector(1)

    def near(c):
        forward(1, c)
        forward(2, c)
        pick(1, c, sel1)

    each(near)
    for i in range(3):
        w_local(i).wait()
        w_arrival(i).wait_recv()
    ffn(1)

    meta_arrival(2).wait_recv()
    sel2 = selector(2)
    pair1 = mixer(1)

    def second(c):
        @pl.when(outer)
        def _():
            r_copy(1, c).wait_recv()
            csend[0, c] = mix(1, c, pair1).astype(jnp.bfloat16)
            cx_copy(c).start()

        pick(2, c, sel2)

    each(second)
    each(lambda c: forward(3, c))
    ffn(2)

    meta_arrival(3).wait_recv()
    sel3 = selector(3)
    pair2 = mixer(2)

    def far(c):
        pick(3, c, sel3)
        give(2, c, pair2)

    each(far)
    ffn(3)
    pair3 = mixer(3)

    @pl.when(outer)
    def _():
        each(lambda c: give(3, c, pair3))
        ffn(0)

    @pl.when(inner)
    def _():
        ffn(0)

        def last_hop(c):
            r_copy(1, c).wait_recv()
            total = mix(1, c, pair1)
            c_copy(1, c).wait_recv()
            csend[0, c] = (total + cmb[src[1], c].astype(jnp.float32)).astype(jnp.bfloat16)
            c_copy(1, c).start()

        give(3, 0, pair3)

        def step(c, carry):
            give(3, c, pair3)
            last_hop(c - 1)
            return carry

        lax.fori_loop(1, CHUNKS, step, 0)
        last_hop(CHUNKS - 1)

    pair0 = mixer(0)

    def finish(c):
        r_copy(0, c).wait_recv()
        total = mix(0, c, pair0)
        remote(
            csend.at[0, c], cmb.at[z, c], c_send.at[0, c], c_recv.at[z, c], zdev(z_in)
        ).wait_recv()
        total = total + cmb[z, c].astype(jnp.float32)

        @pl.when(outer)
        def _():
            out_ref[:, cols(c)] = total.astype(jnp.bfloat16)

        @pl.when(inner)
        def _():
            cx_copy(c).wait_recv()
            out_ref[:, cols(c)] = (total + cmbx[c].astype(jnp.float32)).astype(jnp.bfloat16)

    each(finish)

    def drain(c):
        own_copy(c, 0).wait_send()
        for k in range(LINE):
            y_copy(k, c).wait_send()
            r_copy(k, c).wait_send()
        for k in (2, 3):
            c_copy(k, c).wait_send()

        @pl.when(inner)
        def _():
            own_copy(c, 1).wait_send()
            for k in (1, 2, 3):
                fwd_copy(k, c).wait_send()
            c_copy(1, c).wait_send()

        @pl.when(outer)
        def _():
            cx_copy(c).wait_send()

    each(drain)
    for d in range(1, LINE):
        meta_copy(d).wait_send()
    for i in range(3):
        w_remote(i).wait_send()


def fused(tokens, routes, gates, w_gate, w_up, w_down):
    rows, features = tokens.shape
    experts = lax.axis_size("expert")
    half, width = rows // 2, features // CHUNKS
    hidden = w_gate.shape[2]
    bf16, dma = jnp.bfloat16, pltpu.SemaphoreType.DMA
    return pl.pallas_call(
        moe_kernel,
        out_shape=jax.ShapeDtypeStruct((rows, features), bf16),
        in_specs=[
            pl.BlockSpec(memory_space=pl.ANY),
            pl.BlockSpec(memory_space=pltpu.VMEM),
            pl.BlockSpec(memory_space=pltpu.VMEM),
            pl.BlockSpec(memory_space=pl.ANY),
            pl.BlockSpec(memory_space=pl.ANY),
            pl.BlockSpec(memory_space=pl.ANY),
        ],
        out_specs=pl.BlockSpec(memory_space=pltpu.VMEM),
        scratch_shapes=[
            pltpu.VMEM((LINE, CHUNKS, rows, width), bf16),
            pltpu.VMEM((LINE, 2 * experts, rows), jnp.float32),
            pltpu.VMEM((LINE, rows, features), bf16),
            pltpu.VMEM((LINE, CHUNKS, half, width), bf16),
            pltpu.VMEM((LINE, CHUNKS, rows, width), bf16),
            pltpu.VMEM((LINE, CHUNKS, half, width), bf16),
            pltpu.VMEM((LINE - 1, CHUNKS, rows, width), bf16),
            pltpu.VMEM((LINE, CHUNKS, rows, width), bf16),
            pltpu.VMEM((CHUNKS, rows, width), bf16),
            pltpu.VMEM((2, hidden, features), bf16),
            pltpu.VMEM((2, hidden, features), bf16),
            pltpu.VMEM((2, hidden, features), bf16),
            pltpu.VMEM((2, rows, hidden), bf16),
            dma((2, CHUNKS)),
            dma((LINE - 1, CHUNKS)),
            dma((LINE, CHUNKS)),
            dma((CHUNKS,)),
            dma((LINE - 1,)),
            dma((LINE,)),
            dma((3,)),
            dma((3,)),
            dma((3,)),
            dma((LINE, CHUNKS)),
            dma((LINE, CHUNKS)),
            dma((LINE, CHUNKS)),
            dma((LINE, CHUNKS)),
            dma((LINE - 1, CHUNKS)),
            dma((LINE, CHUNKS)),
            dma((CHUNKS,)),
        ],
        compiler_params=pltpu.CompilerParams(
            collective_id=0, has_side_effects=True, vmem_limit_bytes=56 * 1024 * 1024
        ),
        name="moe",
    )(tokens, routes.T, gates.T, w_gate[0].T, w_up[0].T, w_down[0])


def swiglu(row_block, gate_proj, up_proj):
    gate_act = jnp.dot(row_block, gate_proj, preferred_element_type=jnp.float32)
    up_act = jnp.dot(row_block, up_proj, preferred_element_type=jnp.float32)
    return (jax.nn.silu(gate_act) * up_act).astype(jnp.bfloat16)


def rounded_term(hidden, down_proj):
    return jnp.dot(hidden, down_proj, preferred_element_type=jnp.float32).astype(jnp.bfloat16)


def on_device(tokens, routes, gates, w_gate, w_up, w_down):
    tok_dev, features = tokens.shape
    experts = lax.axis_size("expert")
    capacity = max(5 * tok_dev // 16, TOPK * tok_dev // experts)
    gate_proj = w_gate[0]
    up_proj = w_up[0]
    down_proj = w_down[0]
    pair_expert = routes.reshape(-1)
    onehot = (pair_expert[:, None] == jnp.arange(experts, dtype=jnp.int32)[None, :]).astype(
        jnp.int32
    )
    rank_in = jnp.sum((jnp.cumsum(onehot, axis=0) - onehot) * onehot, axis=1)
    slot_index = (pair_expert * capacity + rank_in).reshape(tok_dev, TOPK)
    all_slots = jnp.arange(experts * capacity, dtype=jnp.int32)
    selector = jnp.any(slot_index[None, :, :] == all_slots[:, None, None], axis=2).astype(
        jnp.bfloat16
    )
    outgoing = jnp.dot(selector, tokens, preferred_element_type=jnp.float32).astype(jnp.bfloat16)
    outgoing = outgoing.reshape(experts, capacity, features)
    arrived = lax.all_to_all(outgoing, "expert", split_axis=0, concat_axis=0, tiled=True)
    hidden = swiglu(
        lax.all_gather(arrived.reshape(experts * capacity, features), "tensor", axis=0, tiled=True),
        gate_proj,
        up_proj,
    )
    term = lax.optimization_barrier(rounded_term(hidden, down_proj))
    summed = lax.psum_scatter(
        term.astype(jnp.float32).astype(jnp.bfloat16), "tensor", scatter_dimension=0, tiled=True
    )
    outputs = summed.reshape(experts, capacity, features)
    returned = lax.all_to_all(outputs, "expert", split_axis=0, concat_axis=0, tiled=True)
    weights = gates.astype(jnp.float32)
    weights = weights / jnp.sum(weights, axis=1, keepdims=True)
    flat_back = returned.reshape(experts * capacity, features)
    picked = jnp.take(flat_back, slot_index.reshape(-1), axis=0).reshape(tok_dev, TOPK, features)
    mixed = jnp.sum(picked.astype(jnp.float32) * weights[:, :, None], axis=1)
    return mixed.astype(jnp.bfloat16)


def solution(mesh):
    in_specs = (
        P(("groups", "expert", "tensor"), None),
        P(("groups", "expert", "tensor"), None),
        P(("groups", "expert", "tensor"), None),
        P("expert", None, "tensor"),
        P("expert", None, "tensor"),
        P("expert", "tensor", None),
    )
    out_specs = P(("groups", "expert", "tensor"), None)
    paired = mesh.shape["expert"] == 2 * LINE and mesh.shape["tensor"] == 2
    return jax.shard_map(
        fused if paired else on_device, mesh=mesh, in_specs=in_specs, out_specs=out_specs, check_vma=False
    )
```
